32 devices in a mesh: ctx: 8 (over z, x), head: 4 (over y, core).
Axes of the slice: x: 2, y: 2, z: 4, core: 2. Of those that a mesh axis runs over, the one named last changes fastest.
Arguments:
- queries: bfloat16 [16384, 2048], P('ctx', 'head'), may hold values from -6 to 6
- keys: bfloat16 [16384, 2048], P('ctx', 'head'), may hold values from -6 to 6
- values: bfloat16 [16384, 4096], P('ctx', 'head'), may hold values from -6 to 6
- gate_pre: float32 [2, 8, 16384], P(None, None, ('ctx', 'head')), may hold values from -8 to 320
Outputs:
- hidden: bfloat16 [16384, 4096], P('ctx', 'head')
- closing_memory: float32 [8, 256, 512], P('head', 'ctx')
- final_norm: float32 [8, 256], P('head')
- final_max: float32 [8], P('head')
The draws below stay inside these ranges and needn't reach their ends.
All inputs are finite; a program needn't handle non-finite values.
Results may differ from the reference program's by a relative error of at most 0.004.
Values sent between devices are 32-bit elements; how exact they have to be, the bound alone decides.
A program may use at most 128 MiB of HBM per device.

```python
import jax
import jax.numpy as jnp
from jax import lax

HEAD_COUNT = 8
DQK = 256
DV = 512
TOK_DEV = 2048
BLK = 512
PROMPT_TOKENS = 16384


def draw_gate_pre(key, part):
    keys = jax.random.split(jax.random.fold_in(key, 17), 10)
    row_entries = jnp.arange(HEAD_COUNT)[:, None]
    base = jnp.clip(1.5 * jax.random.normal(keys[0], (HEAD_COUNT, PROMPT_TOKENS), jnp.float32), -8.0, 8.0)
    base = base.at[:, 1].set(-8.0)
    share = 0.5
    fast = jax.random.bernoulli(keys[4], share, (HEAD_COUNT,))
    fast_rate = jax.random.uniform(keys[5], (HEAD_COUNT,), jnp.float32, 1.0 / 50.0, 1.0 / 30.0)
    rate = jnp.where(fast, fast_rate, 0.5 / PROMPT_TOKENS)
    regions = jnp.exp(jax.random.uniform(keys[6], (HEAD_COUNT, PROMPT_TOKENS // TOK_DEV), jnp.float32, -0.7, 0.7))
    regions = jnp.repeat(regions, TOK_DEV, axis=1)
    rough = jnp.exp(jax.random.uniform(keys[7], (HEAD_COUNT, PROMPT_TOKENS), jnp.float32, -0.7, 0.7))
    forget_decay = rate[:, None] * regions * rough
    spike_position = jax.random.randint(keys[8], (HEAD_COUNT, 3), 0, PROMPT_TOKENS)
    spike_input = jax.random.uniform(keys[9], (HEAD_COUNT, 3), jnp.float32, 0.22, 0.51)
    forget_decay = forget_decay.at[row_entries, spike_position].set(spike_input)
    forget = -jnp.log(jnp.expm1(forget_decay))
    return jnp.stack([base, forget], axis=0).astype(jnp.float32)


def block_levels(stream_key, shape, cuts, smallest, largest):
    level = 1.0
    for dim, blocks in cuts:
        draws = jax.random.uniform(jax.random.fold_in(jax.random.fold_in(stream_key, 6), dim), (blocks,), jnp.float32, smallest / len(cuts), largest / len(cuts))
        level = level * jnp.repeat(jnp.exp(draws), shape[dim] // blocks).reshape((-1,) + (1,) * (len(shape) - 1 - dim))
    return level


def scatter_about(own_key, shape, spread, most, shards=(), kind=jnp.bfloat16):
    loudness = block_levels(own_key, shape, shards, -0.22, 0.18) if shards else 1.0
    values = jax.random.normal(own_key, shape, jnp.float32) * spread * loudness
    return jnp.minimum(jnp.maximum(values, -most), most).astype(kind)


def setup_inputs(seed: int = 0) -> dict:
    key_of = jax.random.split(jax.random.key(seed), 5)
    queries = scatter_about(key_of[0], (PROMPT_TOKENS, HEAD_COUNT * DQK), 1.0, 6.0, ((0, 8), (1, 4)))
    keys = scatter_about(key_of[1], (PROMPT_TOKENS, HEAD_COUNT * DQK), 1.0, 6.0, ((0, 8), (1, 4)))
    values = scatter_about(key_of[2], (PROMPT_TOKENS, HEAD_COUNT * DV), 1.0, 6.0, ((0, 8), (1, 4)))
    gate_pre = draw_gate_pre(jax.random.fold_in(key_of[4], 71), 0)
    return {"queries": queries, "keys": keys, "values": values, "gate_pre": gate_pre}


NEG = -1.0e30


def block_step(carry, inputs):
    memory, normal, stab, offset = carry
    q_block, key_block, v_block, in_gate, forget = inputs
    length = q_block.shape[0]
    scale = q_block.shape[1] ** -0.5
    log_forget = jax.nn.log_sigmoid(forget)
    cum = jnp.cumsum(log_forget)
    whole = cum[-1]
    places = jnp.arange(length, dtype=jnp.int32)
    causal = places[:, None] >= places[None, :]
    log_weight = jnp.where(causal, cum[:, None] - cum[None, :] + in_gate[None, :], NEG)
    top = jnp.maximum(cum + stab, jnp.max(log_weight, axis=1))
    weights = jnp.where(causal, jnp.exp(log_weight - top[:, None]), 0.0)
    scores = jnp.dot(q_block, key_block.T, preferred_element_type=jnp.float32) * scale
    mixed = weights * scores
    denom = jnp.sum(mixed, axis=1)
    numer = jnp.dot(mixed.astype(jnp.bfloat16), v_block, preferred_element_type=jnp.float32)
    carried = jnp.exp(cum + stab - top)
    q_float = q_block.astype(jnp.float32)
    numer = numer + carried[:, None] * jnp.dot(q_float, memory, precision=lax.Precision.HIGHEST)
    denom = denom + carried * jnp.dot(q_float, normal, precision=lax.Precision.HIGHEST)
    new_stab = jnp.maximum(whole + stab, jnp.max(whole - cum + in_gate))
    keep = jnp.exp(whole + stab - new_stab)
    taken = jnp.exp(whole - cum + in_gate - new_stab)
    k_float = key_block.astype(jnp.float32) * scale * taken[:, None]
    memory = keep * memory + jnp.dot(k_float.T, v_block.astype(jnp.float32), precision=lax.Precision.HIGHEST)
    normal = keep * normal + jnp.sum(k_float, axis=0)
    return (memory, normal, new_stab, offset + whole), (numer, denom, top, cum + offset)


def one_head(args):
    q_head, k_head, v_head, in_gate, forget = args
    count = q_head.shape[0] // BLK
    blocks = (q_head.reshape(count, BLK, DQK), k_head.reshape(count, BLK, DQK),
              v_head.reshape(count, BLK, DV), in_gate.reshape(count, BLK), forget.reshape(count, BLK))
    start = (jnp.zeros((DQK, DV), jnp.float32), jnp.zeros((DQK,), jnp.float32),
             jnp.full((), NEG, jnp.float32), jnp.zeros((), jnp.float32))
    final, outs = lax.scan(block_step, start, blocks)
    numer, denom, top, cum = outs
    result = numer / jnp.maximum(jnp.abs(denom), 1.0)[..., None]
    return result.reshape(q_head.shape[0], DV).astype(jnp.bfloat16), final[0], final[1], final[2]


def reference(queries, keys, values, gate_pre):
    q_heads = queries.reshape(PROMPT_TOKENS, HEAD_COUNT, DQK).transpose(1, 0, 2)
    k_heads = keys.reshape(PROMPT_TOKENS, HEAD_COUNT, DQK).transpose(1, 0, 2)
    v_heads = values.reshape(PROMPT_TOKENS, HEAD_COUNT, DV).transpose(1, 0, 2)
    hidden, memory, normal, stab = lax.map(one_head, (q_heads, k_heads, v_heads, gate_pre[0], gate_pre[1]))
    hidden = hidden.transpose(1, 0, 2).reshape(PROMPT_TOKENS, HEAD_COUNT * DV)
    return hidden, memory, normal, stab
```

```python
import functools

import jax
import jax.numpy as jnp
from jax import lax
from jax.experimental import pallas as pl
from jax.experimental.pallas import tpu as pltpu
from jax.sharding import PartitionSpec as P

NEG = -1e30
CW = 128
MESH = pl.DeviceIdType.MESH
F32 = jnp.float32
BF16 = jnp.bfloat16


def shifted(v, k, lane, fill):
    return jnp.where(lane >= k, pltpu.roll(v, k, axis=1), fill)


def kernel(
    nc, nh, hh, toks, dqk, dv,
    q_hbm, k_hbm, v_hbm, g_hbm,
    out_hbm, clos_out, norm_out, max_out,
    q_v, k_v, v_v, g_v, gsend, grecv, ig_s, fg_s,
    a3, mcolb, w3, slp3, insr3, sg3, ng3, norm8, mst, st, norm_st,
    summ, fac, sbuf, srecv, erecv, eout, xsend, xrecv, own, closb, inm,
    numn, cinb, outb,
    in_sem, gs_sem, gr_sem, ss_sem, sr_sem, xs_sem, xr_sem,
    es_sem, er_sem, fs_sem, fr_sem, cs_sem, cr_sem, out_sem,
):
    c = lax.axis_index("ctx")
    hd = lax.axis_index("head")
    i = c // 2
    x = c - 2 * i
    pairs = nc // 2
    L = toks // nh
    R = dqk // nc
    cph = dv // CW
    nu = hh * cph
    nt = hh * nh
    scale = dqk ** (-0.5)

    g_copy = pltpu.make_async_copy(g_hbm, g_v, in_sem.at[0])
    g_copy.start()
    loads = []
    for h in range(hh):
        kc = pltpu.make_async_copy(
            k_hbm.at[:, h * dqk:(h + 1) * dqk], k_v.at[h], in_sem.at[1 + 3 * h])
        vc = pltpu.make_async_copy(
            v_hbm.at[:, h * dv:(h + 1) * dv], v_v.at[h], in_sem.at[2 + 3 * h])
        qc = pltpu.make_async_copy(
            q_hbm.at[:, h * dqk:(h + 1) * dqk], q_v.at[h], in_sem.at[3 + 3 * h])
        loads.append((kc, vc, qc))
    for h in range(hh):
        loads[h][0].start()
        loads[h][1].start()
    for h in range(hh):
        loads[h][2].start()

    barrier = pltpu.get_barrier_semaphore()
    for d in range(1, nh):
        pl.semaphore_signal(barrier, inc=1, device_id=(c, lax.rem(hd + d, nh)), device_id_type=MESH)
    for d in range(1, nc):
        pl.semaphore_signal(barrier, inc=1, device_id=(lax.rem(c + d, nc), hd), device_id_type=MESH)
    g_copy.wait()
    for p in range(nh):
        gsend[p, 0:hh, :] = g_v[0, p * hh:(p + 1) * hh, :]
        gsend[p, hh:2 * hh, :] = g_v[1, p * hh:(p + 1) * hh, :]
    pl.semaphore_wait(barrier, nh - 1 + nc - 1)

    def gate_copy(d):
        to = lax.rem(hd + d, nh)
        return pltpu.make_async_remote_copy(
            src_ref=gsend.at[to], dst_ref=grecv.at[hd], send_sem=gs_sem.at[d],
            recv_sem=gr_sem.at[d], device_id=(c, to), device_id_type=MESH)

    def gate_wait(d):
        frm = lax.rem(hd + nh - d, nh)
        return pltpu.make_async_remote_copy(
            src_ref=gsend.at[frm], dst_ref=grecv.at[frm], send_sem=gs_sem.at[d],
            recv_sem=gr_sem.at[d], device_id=(c, frm), device_id_type=MESH)

    for d in range(1, nh):
        gate_copy(d).start()
    grecv[hd] = gsend[hd]
    for d in range(1, nh):
        gate_wait(d).wait_recv()
    for p in range(nh):
        ig_s[p * hh:(p + 1) * hh, :] = grecv[p, 0:hh, :]
        fg_s[p * hh:(p + 1) * hh, :] = grecv[p, hh:2 * hh, :]
    ig = ig_s[...]
    fg = fg_s[...]
    logf = jnp.minimum(fg, 0.0) - jnp.log1p(jnp.exp(-jnp.abs(fg)))
    lane = lax.broadcasted_iota(jnp.int32, (nt, L), 1)
    cum = logf
    k = 1
    while k < L:
        cum = cum + shifted(cum, k, lane, 0.0)
        k *= 2
    a = ig - cum
    amax_run = a
    k = 1
    while k < L:
        amax_run = jnp.maximum(amax_run, shifted(amax_run, k, lane, NEG))
        k *= 2
    gb = jnp.broadcast_to(cum[:, L - 1:L], (nt, 128))
    ab = jnp.broadcast_to(amax_run[:, L - 1:L], (nt, 128))
    sl = jnp.full((hh, 128), NEG, F32)
    cg = jnp.zeros((hh, 128), F32)
    before, after, gone, keep = [], [], [], []
    for j in range(nh):
        gj = gb[j * hh:(j + 1) * hh]
        new = gj + jnp.maximum(sl, ab[j * hh:(j + 1) * hh])
        before.append(sl)
        gone.append(cg)
        keep.append(jnp.exp(gj + sl - new))
        sl = new
        cg = cg + gj
        after.append(sl)
    slp8 = jnp.concatenate(before, axis=0)
    cg8 = jnp.concatenate(gone, axis=0)
    w = jnp.exp(a + (gb - jnp.concatenate(after, axis=0))[:, 0:1]) * scale
    for r in range(nt):
        a3[r] = a[r:r + 1, :]
        w3[r] = w[r:r + 1, :]
        slp3[r] = slp8[r:r + 1, :]

    def s_copy(u):
        return pltpu.make_async_remote_copy(
            src_ref=sbuf.at[1 - x, u], dst_ref=srecv.at[u], send_sem=xs_sem.at[u],
            recv_sem=xr_sem.at[u], device_id=(2 * i + 1 - x, hd), device_id_type=MESH)

    for h in range(hh):
        loads[h][0].wait()
        loads[h][1].wait()
        mst[h] = jnp.zeros((dqk, dv), BF16)
        norm8[h:h + 1, :] = jnp.zeros((1, dqk), F32)
        for j in range(nh):
            r = j * hh + h
            kt = k_v[h, j * L:(j + 1) * L, :].T.astype(F32)
            kw = kt * w3[r]
            part = kw[:, 0:128]
            for b in range(1, L // 128):
                part = part + kw[:, b * 128:(b + 1) * 128]
            nrow = jnp.sum(part.T, axis=0, keepdims=True)
            upd = jnp.dot(kw.astype(BF16), v_v[h, j * L:(j + 1) * L, :], preferred_element_type=F32)
            if j > 0:
                kp = keep[j][h:h + 1, 0:1]
                upd = upd + kp * st[...]
                nrow = nrow + kp * norm_st[...]
            if j < nh - 1:
                st[...] = upd
                norm_st[...] = nrow
                mst[(j + 1) * hh + h] = upd.astype(BF16)
                norm8[(j + 1) * hh + h:(j + 1) * hh + h + 1, :] = nrow
            else:
                for cc in range(cph):
                    for b in range(pairs):
                        for xx in range(2):
                            r0 = (2 * b + xx) * R
                            sbuf[xx, h * cph + cc, b * R:(b + 1) * R, :] = upd[
                                r0:r0 + R, cc * CW:(cc + 1) * CW]
                    s_copy(h * cph + cc).start()
                summ[c, h:h + 1, :] = nrow
    wide = jnp.ones((1, dqk), F32)
    summ[c, hh:2 * hh, :] = cg[:, 0:1] * wide
    summ[c, 2 * hh:3 * hh, :] = sl[:, 0:1] * wide

    def sum_copy(d, slot):
        return pltpu.make_async_remote_copy(
            src_ref=summ.at[slot], dst_ref=summ.at[slot], send_sem=ss_sem.at[d],
            recv_sem=sr_sem.at[d], device_id=(lax.rem(c + d, nc), hd), device_id_type=MESH)

    for d in range(1, nc):
        sum_copy(d, c).start()

    @pl.when(i == 0)
    def _():
        erecv[...] = jnp.zeros(erecv.shape, F32)

    @pl.when(c == 0)
    def _():
        xrecv[...] = jnp.zeros(xrecv.shape, F32)

    for d in range(1, nc):
        sum_copy(d, lax.rem(c + nc - d, nc)).wait_recv()

    stab = jnp.full((hh, dqk), NEG, F32)
    norm = jnp.zeros((hh, dqk), F32)
    zero = jnp.zeros((hh, dqk), F32)
    in_stab, in_norm = zero, zero
    fa = [zero, zero, zero, zero]
    for s in range(nc):
        total = summ[s, hh:2 * hh, :]
        late = summ[s, 2 * hh:3 * hh, :]
        in_stab = jnp.where(c == s, stab, in_stab)
        in_norm = jnp.where(c == s, norm, in_norm)
        new = jnp.maximum(stab + total, late)
        fe = jnp.exp(stab + total - new)
        fl = jnp.exp(late - new)
        o = 2 * (s % 2)
        fa[o] = jnp.where(i == s // 2, fe, fa[o])
        fa[o + 1] = jnp.where(i == s // 2, fl, fa[o + 1])
        norm = fe * norm + fl * summ[s, 0:hh, :]
        stab = new
    norm_out[...] = norm
    max_out[...] = stab[:, 0:128]
    for h in range(hh):
        for o in range(4):
            fac[h, o:o + 1, :] = fa[o][h:h + 1, 0:128]
    insr8 = jnp.concatenate([in_stab[:, 0:128]] * nh, axis=0) + cg8
    sg8 = jnp.maximum(slp8, insr8)
    m = jnp.maximum(amax_run, sg8[:, 0:1])
    ng = (jnp.exp(slp8 - sg8)[:, 0:1] * norm8[...]
          + jnp.exp(insr8 - sg8)[:, 0:1] * jnp.concatenate([in_norm] * nh, axis=0))
    mt = m.T
    for r in range(nt):
        insr3[r] = insr8[r:r + 1, :]
        sg3[r] = sg8[r:r + 1, :]
        ng3[r] = ng[r:r + 1, :]
        mcolb[r] = jnp.broadcast_to(mt[:, r:r + 1], (L, 128))
    for h in range(hh):
        loads[h][2].wait()

    tt = min(256, L)

    def intra(task):
        h = task // nh
        j = task - h * nh
        r = j * hh + h
        base = pl.multiple_of(j * L, L)
        for rt in range(L // tt):
            t0 = rt * tt
            ncol = t0 + tt
            rows = pl.ds(pl.multiple_of(base + t0, tt), tt)
            q = q_v[h, rows, :]
            mc = mcolb[r, t0:t0 + tt, :]
            kk = k_v[h, pl.ds(base, ncol), :]
            vv = v_v[h, pl.ds(base, ncol), :]
            s = lax.dot_general(q, kk, (((1,), (1,)), ((), ())), preferred_element_type=F32)
            e = jnp.exp(a3[r][:, 0:ncol] - mc[:, 0:1])
            ti = lax.broadcasted_iota(jnp.int32, (tt, ncol), 0) + t0
            si = lax.broadcasted_iota(jnp.int32, (tt, ncol), 1)
            mixed = jnp.where(ti >= si, e, 0.0) * (s * scale)
            qn = jnp.sum(q.astype(F32) * ng3[r], axis=1, keepdims=True)
            den = jnp.sum(mixed, axis=1, keepdims=True) + jnp.exp(sg3[r] - mc)[:, 0:1] * qn
            inv = 1.0 / jnp.maximum(jnp.abs(den), 1.0)
            num = jnp.dot(mixed.astype(BF16), vv, preferred_element_type=F32)
            loc = jnp.dot(q, mst[r], preferred_element_type=F32)
            num = num * inv + (jnp.exp(slp3[r] - mc)[:, 0:1] * inv) * loc
            for cc in range(cph):
                numn[h * cph + cc, rows, :] = num[:, cc * CW:(cc + 1) * CW]
            cinb[h, rows, :] = jnp.exp(insr3[r] - mc) * inv

    def e_copy(u):
        to = lax.rem(c + 2, nc)
        return pltpu.make_async_remote_copy(
            src_ref=eout.at[u], dst_ref=erecv.at[u], send_sem=es_sem.at[u],
            recv_sem=er_sem.at[u], device_id=(to, hd), device_id_type=MESH)

    def f_copy(u):
        return pltpu.make_async_remote_copy(
            src_ref=xsend.at[u], dst_ref=xrecv.at[u], send_sem=fs_sem.at[u],
            recv_sem=fr_sem.at[u], device_id=(2 * i + 1 - x, hd), device_id_type=MESH)

    def c_copy(u, b):
        return pltpu.make_async_remote_copy(
            src_ref=eout.at[u, pl.ds(b * R, R), :], dst_ref=closb.at[u],
            send_sem=cs_sem.at[u, b], recv_sem=cr_sem.at[u],
            device_id=(2 * b + x, hd), device_id_type=MESH)

    per = nt // nu

    def step(u, carry):
        for o in range(per):
            intra(u * per + o)
        h = u // cph
        s_copy(u).wait_recv()

        @pl.when(i > 0)
        def _():
            e_copy(u).wait_recv()

        mine = sbuf[x, u]
        other = srecv[u]
        e = erecv[u]
        f = fac[h]
        first = jnp.where(x == 0, mine, other)
        second = jnp.where(x == 0, other, mine)
        mid = f[0:1, :] * e + f[1:2, :] * first
        eout[u] = f[2:3, :] * mid + f[3:4, :] * second
        xsend[u] = jnp.where(x == 0, mid, e)
        own[u] = jnp.where(x == 0, e, mid)

        @pl.when(i < pairs - 1)
        def _():
            e_copy(u).start()

        @pl.when(c != 1)
        def _():
            f_copy(u).start()

        @pl.when(i == pairs - 1)
        def _():
            for b in range(pairs - 1):
                c_copy(u, b).start()
            closb[u] = eout[u, (pairs - 1) * R:pairs * R, :]

        return carry

    lax.fori_loop(0, nu, step, 0)

    rt = min(512, toks)

    def out_copy(u):
        return pltpu.make_async_copy(
            outb.at[u], out_hbm.at[:, pl.ds(pl.multiple_of(u * CW, CW), CW)], out_sem.at[u])

    def final(u, carry):
        h = u // cph

        @pl.when(c > 0)
        def _():
            f_copy(u).wait_recv()

        inm[:, x] = own[u].reshape(pairs, R, CW)
        inm[:, 1 - x] = xrecv[u].reshape(pairs, R, CW)
        mem = inm[...].reshape(dqk, CW).astype(BF16)
        for b in range(toks // rt):
            rows = pl.ds(b * rt, rt)
            got = jnp.dot(q_v[h, rows, :], mem, preferred_element_type=F32)
            outb[u, rows, :] = (numn[u, rows, :] + cinb[h, rows, :] * got).astype(BF16)
        out_copy(u).start()
        return carry

    lax.fori_loop(0, nu, final, 0)

    for u in range(nu):
        @pl.when(i < pairs - 1)
        def _():
            c_copy(u, i).wait_recv()

        h, cc = u // cph, u % cph
        clos_out[h, :, cc * CW:(cc + 1) * CW] = closb[u]

    for d in range(1, nh):
        gate_copy(d).wait_send()
    for d in range(1, nc):
        sum_copy(d, c).wait_send()

    def drain(u, carry):
        s_copy(u).wait_send()

        @pl.when(i < pairs - 1)
        def _():
            e_copy(u).wait_send()

        @pl.when(c != 1)
        def _():
            f_copy(u).wait_send()

        @pl.when(i == pairs - 1)
        def _():
            for b in range(pairs - 1):
                c_copy(u, b).wait_send()

        out_copy(u).wait()
        return carry

    lax.fori_loop(0, nu, drain, 0)


def on_device(nc, nh, queries, keys, values, gate_pre):
    toks = queries.shape[0]
    hh = gate_pre.shape[1] // nh
    dqk = queries.shape[1] // hh
    dv = values.shape[1] // hh
    L = toks // nh
    R = dqk // nc
    pairs = nc // 2
    nu = hh * dv // CW
    nt = hh * nh
    half = dqk // 2
    vm = pltpu.VMEM
    dma = pltpu.SemaphoreType.DMA
    anyspec = pl.BlockSpec(memory_space=pl.ANY)
    vspec = pl.BlockSpec(memory_space=pltpu.VMEM)
    macs = hh * toks * (L * (dqk + dv) + 3 * dqk * dv)
    hidden, closing, norm, top = pl.pallas_call(
        functools.partial(kernel, nc, nh, hh, toks, dqk, dv),
        out_shape=(
            jax.ShapeDtypeStruct((toks, hh * dv), BF16),
            jax.ShapeDtypeStruct((hh, R, dv), F32),
            jax.ShapeDtypeStruct((hh, dqk), F32),
            jax.ShapeDtypeStruct((hh, 128), F32),
        ),
        in_specs=[anyspec] * 4,
        out_specs=(anyspec, vspec, vspec, vspec),
        scratch_shapes=[
            vm((hh, toks, dqk), BF16), vm((hh, toks, dqk), BF16), vm((hh, toks, dv), BF16),
            vm(gate_pre.shape, F32), vm((nh, 8, L), F32), vm((nh, 8, L), F32),
            vm((nt, L), F32), vm((nt, L), F32),
            vm((nt, 1, L), F32), vm((nt, L, 128), F32), vm((nt, 1, L), F32),
            vm((nt, 1, 128), F32), vm((nt, 1, 128), F32), vm((nt, 1, 128), F32),
            vm((nt, 1, dqk), F32), vm((nt, dqk), F32), vm((nt, dqk, dv), BF16),
            vm((dqk, dv), F32), vm((1, dqk), F32),
            vm((nc, 8, dqk), F32), vm((hh, 8, 128), F32),
            vm((2, nu, half, CW), F32), vm((nu, half, CW), F32), vm((nu, half, CW), F32),
            vm((nu, half, CW), F32), vm((nu, half, CW), F32), vm((nu, half, CW), F32),
            vm((nu, half, CW), F32), vm((nu, R, CW), F32), vm((pairs, 2, R, CW), F32),
            vm((nu, toks, CW), F32), vm((hh, toks, 128), F32), vm((nu, toks, CW), BF16),
            dma((1 + 3 * hh,)), dma((nh,)), dma((nh,)), dma((nc,)), dma((nc,)),
            dma((nu,)), dma((nu,)), dma((nu,)), dma((nu,)), dma((nu,)), dma((nu,)),
            dma((nu, pairs)), dma((nu,)), dma((nu,)),
        ],
        compiler_params=pltpu.CompilerParams(
            collective_id=0, has_side_effects=True, vmem_limit_bytes=56 * 1024 * 1024),
        cost_estimate=pl.CostEstimate(
            flops=2 * macs, bytes_accessed=12 * 1024 * 1024, transcendentals=hh * toks * L),
        name="mlstm",
    )(queries, keys, values, gate_pre)
    return hidden, closing, norm, top[:, 0]


def solution(mesh):
    nc, nh = mesh.shape["ctx"], mesh.shape["head"]
    in_specs = (
        P("ctx", "head"),
        P("ctx", "head"),
        P("ctx", "head"),
        P(None, None, ("ctx", "head")),
    )
    out_specs = (P("ctx", "head"), P("head", "ctx", None), P("head", None), P("head"))
    return jax.shard_map(
        functools.partial(on_device, nc, nh),
        mesh=mesh, in_specs=in_specs, out_specs=out_specs, check_vma=False,
    )
```

```python
import functools

import jax
import jax.numpy as jnp
from jax import lax
from jax.experimental import pallas as pl
from jax.experimental.pallas import tpu as pltpu
from jax.sharding import PartitionSpec as P

NEG = -1e30
CW = 128
MESH = pl.DeviceIdType.MESH
F32 = jnp.float32
BF16 = jnp.bfloat16


def shifted(v, k, lane, fill):
    return jnp.where(lane >= k, pltpu.roll(v, k, axis=1), fill)


def kernel(
    nc, nh, hh, toks, dqk, dv,
    q_hbm, k_hbm, v_hbm, g_hbm,
    num_hbm, qs_hbm, mem_out, clos_out, norm_out, max_out,
    q_v, k_v, v_v, g_v, gsend, grecv, ig_s, fg_s, kt_v, kw_v,
    a3, mcolb, w3, slp3, insr3, sg3, ng3, norm8, mst, st,
    summ, fac, sbuf, srecv, erecv, eout, xsend, xrecv, own, closb, inm,
    numv, qsv,
    in_sem, gs_sem, gr_sem, ss_sem, sr_sem, xs_sem, xr_sem,
    es_sem, er_sem, fs_sem, fr_sem, cs_sem, cr_sem, num_sem, qs_sem,
):
    c = lax.axis_index("ctx")
    hd = lax.axis_index("head")
    i = c // 2
    x = c - 2 * i
    pairs = nc // 2
    L = toks // nh
    R = dqk // nc
    cph = dv // CW
    nu = hh * cph
    nt = hh * nh
    scale = dqk ** (-0.5)

    g_copy = pltpu.make_async_copy(g_hbm, g_v, in_sem.at[0])
    g_copy.start()
    loads = []
    for h in range(hh):
        kc = pltpu.make_async_copy(
            k_hbm.at[:, h * dqk:(h + 1) * dqk], k_v.at[h], in_sem.at[1 + 3 * h])
        vc = pltpu.make_async_copy(
            v_hbm.at[:, h * dv:(h + 1) * dv], v_v.at[h], in_sem.at[2 + 3 * h])
        qc = pltpu.make_async_copy(
            q_hbm.at[:, h * dqk:(h + 1) * dqk], q_v.at[h], in_sem.at[3 + 3 * h])
        loads.append((kc, vc, qc))
    for h in range(hh):
        loads[h][0].start()
        loads[h][1].start()
    for h in range(hh):
        loads[h][2].start()

    barrier = pltpu.get_barrier_semaphore()
    for d in range(1, nh):
        pl.semaphore_signal(barrier, inc=1, device_id=(c, lax.rem(hd + d, nh)), device_id_type=MESH)
    for d in range(1, nc):
        pl.semaphore_signal(barrier, inc=1, device_id=(lax.rem(c + d, nc), hd), device_id_type=MESH)
    g_copy.wait()
    for p in range(nh):
        gsend[p, 0:hh, :] = g_v[0, p * hh:(p + 1) * hh, :]
        gsend[p, hh:2 * hh, :] = g_v[1, p * hh:(p + 1) * hh, :]
    pl.semaphore_wait(barrier, nh - 1 + nc - 1)

    def gate_copy(d):
        to = lax.rem(hd + d, nh)
        return pltpu.make_async_remote_copy(
            src_ref=gsend.at[to], dst_ref=grecv.at[hd], send_sem=gs_sem.at[d],
            recv_sem=gr_sem.at[d], device_id=(c, to), device_id_type=MESH)

    def gate_wait(d):
        frm = lax.rem(hd + nh - d, nh)
        return pltpu.make_async_remote_copy(
            src_ref=gsend.at[frm], dst_ref=grecv.at[frm], send_sem=gs_sem.at[d],
            recv_sem=gr_sem.at[d], device_id=(c, frm), device_id_type=MESH)

    for d in range(1, nh):
        gate_copy(d).start()
    grecv[hd] = gsend[hd]
    for h in range(hh):
        loads[h][0].wait()
        for j in range(nh):
            kt_v[j * hh + h] = k_v[h, j * L:(j + 1) * L, :].T
    for d in range(1, nh):
        gate_wait(d).wait_recv()
    for p in range(nh):
        ig_s[p * hh:(p + 1) * hh, :] = grecv[p, 0:hh, :]
        fg_s[p * hh:(p + 1) * hh, :] = grecv[p, hh:2 * hh, :]
    ig = ig_s[...]
    fg = fg_s[...]
    logf = jnp.minimum(fg, 0.0) - jnp.log1p(jnp.exp(-jnp.abs(fg)))
    lane = lax.broadcasted_iota(jnp.int32, (nt, L), 1)
    cum = logf
    k = 1
    while k < L:
        cum = cum + shifted(cum, k, lane, 0.0)
        k *= 2
    a = ig - cum
    gb = jnp.broadcast_to(cum[:, L - 1:L], (nt, 128))
    ab = jnp.broadcast_to(jnp.max(a, axis=1, keepdims=True), (nt, 128))
    sl = jnp.full((hh, 128), NEG, F32)
    cg = jnp.zeros((hh, 128), F32)
    before, after, gone, keep = [], [], [], []
    for j in range(nh):
        gj = gb[j * hh:(j + 1) * hh]
        new = gj + jnp.maximum(sl, ab[j * hh:(j + 1) * hh])
        before.append(sl)
        gone.append(cg)
        keep.append(jnp.exp(gj + sl - new))
        sl = new
        cg = cg + gj
        after.append(sl)
    slp8 = jnp.concatenate(before, axis=0)
    cg8 = jnp.concatenate(gone, axis=0)
    w = jnp.exp(a + (gb - jnp.concatenate(after, axis=0))[:, 0:1]) * scale
    for r in range(nt):
        a3[r] = a[r:r + 1, :]
        w3[r] = w[r:r + 1, :]
        slp3[r] = slp8[r:r + 1, :]

    def s_copy(u):
        return pltpu.make_async_remote_copy(
            src_ref=sbuf.at[1 - x, u], dst_ref=srecv.at[u], send_sem=xs_sem.at[u],
            recv_sem=xr_sem.at[u], device_id=(2 * i + 1 - x, hd), device_id_type=MESH)

    def sum_copy(d, slot):
        return pltpu.make_async_remote_copy(
            src_ref=summ.at[slot], dst_ref=summ.at[slot], send_sem=ss_sem.at[d],
            recv_sem=sr_sem.at[d], device_id=(lax.rem(c + d, nc), hd), device_id_type=MESH)

    for h in range(hh):
        norm8[h:h + 1, :] = jnp.zeros((1, dqk), F32)
        run = None
        for j in range(nh):
            r = j * hh + h
            kw = kt_v[r].astype(F32) * w3[r]
            part = kw[:, 0:128]
            for b in range(1, L // 128):
                part = part + kw[:, b * 128:(b + 1) * 128]
            nrow = jnp.sum(part.T, axis=0, keepdims=True)
            kw_v[r] = kw.astype(BF16)
            run = nrow if j == 0 else nrow + keep[j][h:h + 1, 0:1] * run
            if j < nh - 1:
                norm8[r + hh:r + hh + 1, :] = run
            else:
                summ[c, h:h + 1, :] = run
    wide = jnp.ones((1, dqk), F32)
    summ[c, hh:2 * hh, :] = cg[:, 0:1] * wide
    summ[c, 2 * hh:3 * hh, :] = sl[:, 0:1] * wide
    for d in range(1, nc):
        sum_copy(d, c).start()

    for h in range(hh):
        loads[h][1].wait()
        mst[h] = jnp.zeros((dqk, dv), BF16)
        for j in range(nh):
            r = j * hh + h
            upd = jnp.dot(kw_v[r], v_v[h, j * L:(j + 1) * L, :], preferred_element_type=F32)
            if j > 0:
                upd = upd + keep[j][h:h + 1, 0:1] * st[...]
            if j < nh - 1:
                st[...] = upd
                mst[r + hh] = upd.astype(BF16)
            else:
                for cc in range(cph):
                    for b in range(pairs):
                        for xx in range(2):
                            r0 = (2 * b + xx) * R
                            sbuf[xx, h * cph + cc, b * R:(b + 1) * R, :] = upd[
                                r0:r0 + R, cc * CW:(cc + 1) * CW]
                    s_copy(h * cph + cc).start()

    amax_run = a
    k = 1
    while k < L:
        amax_run = jnp.maximum(amax_run, shifted(amax_run, k, lane, NEG))
        k *= 2

    @pl.when(i == 0)
    def _():
        erecv[...] = jnp.zeros(erecv.shape, F32)

    @pl.when(c == 0)
    def _():
        xrecv[...] = jnp.zeros(xrecv.shape, F32)

    for d in range(1, nc):
        sum_copy(d, lax.rem(c + nc - d, nc)).wait_recv()

    stab = jnp.full((hh, dqk), NEG, F32)
    norm = jnp.zeros((hh, dqk), F32)
    zero = jnp.zeros((hh, dqk), F32)
    in_stab, in_norm = zero, zero
    fa = [zero, zero, zero, zero]
    for s in range(nc):
        total = summ[s, hh:2 * hh, :]
        late = summ[s, 2 * hh:3 * hh, :]
        in_stab = jnp.where(c == s, stab, in_stab)
        in_norm = jnp.where(c == s, norm, in_norm)
        new = jnp.maximum(stab + total, late)
        fe = jnp.exp(stab + total - new)
        fl = jnp.exp(late - new)
        o = 2 * (s % 2)
        fa[o] = jnp.where(i == s // 2, fe, fa[o])
        fa[o + 1] = jnp.where(i == s // 2, fl, fa[o + 1])
        norm = fe * norm + fl * summ[s, 0:hh, :]
        stab = new
    norm_out[...] = norm
    max_out[...] = stab[:, 0:128]
    for h in range(hh):
        for o in range(4):
            fac[h, o:o + 1, :] = fa[o][h:h + 1, 0:128]
    insr8 = jnp.concatenate([in_stab[:, 0:128]] * nh, axis=0) + cg8
    sg8 = jnp.maximum(slp8, insr8)
    m = jnp.maximum(amax_run, sg8[:, 0:1])
    ng = (jnp.exp(slp8 - sg8)[:, 0:1] * norm8[...]
          + jnp.exp(insr8 - sg8)[:, 0:1] * jnp.concatenate([in_norm] * nh, axis=0))
    mt = m.T
    for r in range(nt):
        insr3[r] = insr8[r:r + 1, :]
        sg3[r] = sg8[r:r + 1, :]
        ng3[r] = ng[r:r + 1, :]
        mcolb[r] = jnp.broadcast_to(mt[:, r:r + 1], (L, 128))
    for h in range(hh):
        loads[h][2].wait()

    tt = min(256, L)

    def num_copy(task):
        h = task // nh
        rows = pl.ds(pl.multiple_of((task - h * nh) * L, L), L)
        return pltpu.make_async_copy(
            numv.at[h, rows, :], num_hbm.at[h, rows, :], num_sem.at[task])

    def qs_copy(task):
        h = task // nh
        rows = pl.ds(pl.multiple_of((task - h * nh) * L, L), L)
        return pltpu.make_async_copy(
            qsv.at[h, rows, :], qs_hbm.at[h, rows, :], qs_sem.at[task])

    def intra(task, carry):
        h = task // nh
        j = task - h * nh
        r = j * hh + h
        base = pl.multiple_of(j * L, L)
        for rt in range(L // tt):
            t0 = rt * tt
            ncol = t0 + tt
            rows = pl.ds(pl.multiple_of(base + t0, tt), tt)
            q = q_v[h, rows, :]
            mc = mcolb[r, t0:t0 + tt, :]
            kk = kt_v[r, :, 0:ncol]
            vv = v_v[h, pl.ds(base, ncol), :]
            s = jnp.dot(q, kk, preferred_element_type=F32)
            e = jnp.exp(a3[r][:, 0:ncol] - mc[:, 0:1])
            ti = lax.broadcasted_iota(jnp.int32, (tt, ncol), 0) + t0
            si = lax.broadcasted_iota(jnp.int32, (tt, ncol), 1)
            mixed = jnp.where(ti >= si, e, 0.0) * (s * scale)
            qf = q.astype(F32)
            qn = jnp.sum(qf * ng3[r], axis=1, keepdims=True)
            den = jnp.sum(mixed, axis=1, keepdims=True) + jnp.exp(sg3[r] - mc)[:, 0:1] * qn
            inv = 1.0 / jnp.maximum(jnp.abs(den), 1.0)
            num = jnp.dot(mixed.astype(BF16), vv, preferred_element_type=F32)
            loc = jnp.dot(q, mst[r], preferred_element_type=F32)
            num = num * inv + (jnp.exp(slp3[r] - mc)[:, 0:1] * inv) * loc
            numv[h, rows, :] = num.astype(BF16)
            qsv[h, rows, :] = (qf * (jnp.exp(insr3[r] - mc)[:, 0:1] * inv)).astype(BF16)
        num_copy(task).start()
        qs_copy(task).start()
        return carry

    def e_copy(u):
        to = lax.rem(c + 2, nc)
        return pltpu.make_async_remote_copy(
            src_ref=eout.at[u], dst_ref=erecv.at[u], send_sem=es_sem.at[u],
            recv_sem=er_sem.at[u], device_id=(to, hd), device_id_type=MESH)

    def f_copy(u):
        return pltpu.make_async_remote_copy(
            src_ref=xsend.at[u], dst_ref=xrecv.at[u], send_sem=fs_sem.at[u],
            recv_sem=fr_sem.at[u], device_id=(2 * i + 1 - x, hd), device_id_type=MESH)

    def c_copy(u, b):
        return pltpu.make_async_remote_copy(
            src_ref=eout.at[u, pl.ds(b * R, R), :], dst_ref=closb.at[u],
            send_sem=cs_sem.at[u, b], recv_sem=cr_sem.at[u],
            device_id=(2 * b + x, hd), device_id_type=MESH)

    lead = jnp.minimum(i, nt // 2)

    def done(u):
        return jnp.minimum(lead + (u + 1) // 2, nt)

    def step(u, carry):
        lax.fori_loop(jnp.where(u == 0, 0, done(u - 1)), done(u), intra, 0)
        h = u // cph
        s_copy(u).wait_recv()

        @pl.when(i > 0)
        def _():
            e_copy(u).wait_recv()

        mine = sbuf[x, u]
        other = srecv[u]
        e = erecv[u]
        f = fac[h]
        first = jnp.where(x == 0, mine, other)
        second = jnp.where(x == 0, other, mine)
        mid = f[0:1, :] * e + f[1:2, :] * first
        eout[u] = f[2:3, :] * mid + f[3:4, :] * second
        xsend[u] = jnp.where(x == 0, mid, e)
        own[u] = jnp.where(x == 0, e, mid)

        @pl.when(i < pairs - 1)
        def _():
            e_copy(u).start()

        @pl.when(c != 1)
        def _():
            f_copy(u).start()

        @pl.when(i == pairs - 1)
        def _():
            for b in range(pairs - 1):
                c_copy(u, b).start()
            closb[u] = eout[u, (pairs - 1) * R:pairs * R, :]

        return carry

    lax.fori_loop(0, nu, step, 0)

    lax.fori_loop(done(nu - 1), nt, intra, 0)

    def gather(u, carry):
        @pl.when(c > 0)
        def _():
            f_copy(u).wait_recv()

        inm[:, x] = own[u].reshape(pairs, R, CW)
        inm[:, 1 - x] = xrecv[u].reshape(pairs, R, CW)
        mem_out[u] = inm[...].reshape(dqk, CW).astype(BF16)
        return carry

    lax.fori_loop(0, nu, gather, 0)

    for u in range(nu):
        @pl.when(i < pairs - 1)
        def _():
            c_copy(u, i).wait_recv()

        h, cc = u // cph, u % cph
        clos_out[h, :, cc * CW:(cc + 1) * CW] = closb[u]

    for d in range(1, nh):
        gate_copy(d).wait_send()
    for d in range(1, nc):
        sum_copy(d, c).wait_send()

    def drain(u, carry):
        s_copy(u).wait_send()

        @pl.when(i < pairs - 1)
        def _():
            e_copy(u).wait_send()

        @pl.when(c != 1)
        def _():
            f_copy(u).wait_send()

        @pl.when(i == pairs - 1)
        def _():
            for b in range(pairs - 1):
                c_copy(u, b).wait_send()

        return carry

    lax.fori_loop(0, nu, drain, 0)

    def drain_own(task, carry):
        num_copy(task).wait()
        qs_copy(task).wait()
        return carry

    lax.fori_loop(0, nt, drain_own, 0)


def readout(hh, cph, num_ref, qs_ref, mem_ref, clos_in, norm_in, max_in,
            out_ref, clos_out, norm_out, max_out):
    dv = cph * CW
    for h in range(hh):
        mem = jnp.concatenate([mem_ref[h * cph + cc] for cc in range(cph)], axis=1)
        got = jnp.dot(qs_ref[h], mem, preferred_element_type=F32)
        out_ref[:, h * dv:(h + 1) * dv] = (num_ref[h].astype(F32) + got).astype(BF16)

    @pl.when(pl.program_id(0) == 0)
    def _():
        clos_out[...] = clos_in[...]
        norm_out[...] = norm_in[...]
        for h in range(hh):
            max_out[h] = max_in[h, 0]


def on_device(nc, nh, queries, keys, values, gate_pre):
    toks = queries.shape[0]
    hh = gate_pre.shape[1] // nh
    dqk = queries.shape[1] // hh
    dv = values.shape[1] // hh
    L = toks // nh
    R = dqk // nc
    pairs = nc // 2
    nu = hh * dv // CW
    nt = hh * nh
    half = dqk // 2
    vm = pltpu.VMEM
    dma = pltpu.SemaphoreType.DMA
    anyspec = pl.BlockSpec(memory_space=pl.ANY)
    vspec = pl.BlockSpec(memory_space=pltpu.VMEM)
    macs = hh * toks * (L * (dqk + dv) + 3 * dqk * dv)
    num, qs, mem, closing, norm, top = pl.pallas_call(
        functools.partial(kernel, nc, nh, hh, toks, dqk, dv),
        out_shape=(
            jax.ShapeDtypeStruct((hh, toks, dv), BF16),
            jax.ShapeDtypeStruct((hh, toks, dqk), BF16),
            jax.ShapeDtypeStruct((nu, dqk, CW), BF16),
            jax.ShapeDtypeStruct((hh, R, dv), F32),
            jax.ShapeDtypeStruct((hh, dqk), F32),
            jax.ShapeDtypeStruct((hh, 128), F32),
        ),
        in_specs=[anyspec] * 4,
        out_specs=(anyspec, anyspec, vspec, vspec, vspec, vspec),
        scratch_shapes=[
            vm((hh, toks, dqk), BF16), vm((hh, toks, dqk), BF16), vm((hh, toks, dv), BF16),
            vm(gate_pre.shape, F32), vm((nh, 8, L), F32), vm((nh, 8, L), F32),
            vm((nt, L), F32), vm((nt, L), F32), vm((nt, dqk, L), BF16), vm((nt, dqk, L), BF16),
            vm((nt, 1, L), F32), vm((nt, L, 128), F32), vm((nt, 1, L), F32),
            vm((nt, 1, 128), F32), vm((nt, 1, 128), F32), vm((nt, 1, 128), F32),
            vm((nt, 1, dqk), F32), vm((nt, dqk), F32), vm((nt, dqk, dv), BF16),
            vm((dqk, dv), F32),
            vm((nc, 8, dqk), F32), vm((hh, 8, 128), F32),
            vm((2, nu, half, CW), F32), vm((nu, half, CW), F32), vm((nu, half, CW), F32),
            vm((nu, half, CW), F32), vm((nu, half, CW), F32), vm((nu, half, CW), F32),
            vm((nu, half, CW), F32), vm((nu, R, CW), F32), vm((pairs, 2, R, CW), F32),
            vm((hh, toks, dv), BF16), vm((hh, toks, dqk), BF16),
            dma((1 + 3 * hh,)), dma((nh,)), dma((nh,)), dma((nc,)), dma((nc,)),
            dma((nu,)), dma((nu,)), dma((nu,)), dma((nu,)), dma((nu,)), dma((nu,)),
            dma((nu, pairs)), dma((nu,)), dma((nt,)), dma((nt,)),
        ],
        compiler_params=pltpu.CompilerParams(
            collective_id=0, has_side_effects=True, vmem_limit_bytes=56 * 1024 * 1024),
        cost_estimate=pl.CostEstimate(
            flops=2 * macs, bytes_accessed=12 * 1024 * 1024, transcendentals=hh * toks * L),
        name="mlstm",
    )(queries, keys, values, gate_pre)
    tb = min(256, toks)
    return pl.pallas_call(
        functools.partial(readout, hh, dv // CW),
        grid=(toks // tb,),
        out_shape=(
            jax.ShapeDtypeStruct((toks, hh * dv), BF16),
            jax.ShapeDtypeStruct((hh, R, dv), F32),
            jax.ShapeDtypeStruct((hh, dqk), F32),
            jax.ShapeDtypeStruct((hh,), F32),
        ),
        in_specs=[
            pl.BlockSpec((hh, tb, dv), lambda t: (0, t, 0)),
            pl.BlockSpec((hh, tb, dqk), lambda t: (0, t, 0)),
            vspec, vspec, vspec, pl.BlockSpec(memory_space=pltpu.SMEM),
        ],
        out_specs=(
            pl.BlockSpec((tb, hh * dv), lambda t: (t, 0)),
            vspec, vspec, pl.BlockSpec(memory_space=pltpu.SMEM),
        ),
        compiler_params=pltpu.CompilerParams(vmem_limit_bytes=60 * 1024 * 1024),
        cost_estimate=pl.CostEstimate(
            flops=2 * hh * toks * dqk * dv, bytes_accessed=11 * 1024 * 1024, transcendentals=0),
        name="readout",
    )(num, qs, mem, closing, norm, top)


def solution(mesh):
    nc, nh = mesh.shape["ctx"], mesh.shape["head"]
    in_specs = (
        P("ctx", "head"),
        P("ctx", "head"),
        P("ctx", "head"),
        P(None, None, ("ctx", "head")),
    )
    out_specs = (P("ctx", "head"), P("head", "ctx", None), P("head", None), P("head"))
    return jax.shard_map(
        functools.partial(on_device, nc, nh),
        mesh=mesh, in_specs=in_specs, out_specs=out_specs, check_vma=False,
    )
```

```python
import functools

import jax
import jax.numpy as jnp
from jax import lax
from jax.experimental import pallas as pl
from jax.experimental.pallas import tpu as pltpu
from jax.sharding import PartitionSpec as P

NEG = -1e30
CW = 128
MESH = pl.DeviceIdType.MESH
F32 = jnp.float32
BF16 = jnp.bfloat16


def shifted(v, k, lane, fill):
    return jnp.where(lane >= k, pltpu.roll(v, k, axis=1), fill)


def kernel(
    nc, nh, hh, toks, dqk, dv,
    q_hbm, k_hbm, v_hbm, g_hbm,
    numv, qsv, mem_out, clos_out, norm_out, max_out,
    q_v, k_v, v_v, g_v, gsend, grecv, ig_s, fg_s, kt_v, kw_v,
    a3, mcolb, w3, slp3, insr3, sg3, ng3, norm8, mst, st,
    summ, fac, sbuf, srecv, erecv, eout, xsend, xrecv, own, closb, inm,
    in_sem, gs_sem, gr_sem, ss_sem, sr_sem, xs_sem, xr_sem,
    es_sem, er_sem, fs_sem, fr_sem, cs_sem, cr_sem,
):
    c = lax.axis_index("ctx")
    hd = lax.axis_index("head")
    i = c // 2
    x = c - 2 * i
    pairs = nc // 2
    L = toks // nh
    R = dqk // nc
    cph = dv // CW
    nu = hh * cph
    nt = hh * nh
    scale = dqk ** (-0.5)

    g_copy = pltpu.make_async_copy(g_hbm, g_v, in_sem.at[0])
    g_copy.start()
    loads = []
    for h in range(hh):
        kc = pltpu.make_async_copy(
            k_hbm.at[:, h * dqk:(h + 1) * dqk], k_v.at[h], in_sem.at[1 + 3 * h])
        vc = pltpu.make_async_copy(
            v_hbm.at[:, h * dv:(h + 1) * dv], v_v.at[h], in_sem.at[2 + 3 * h])
        qc = pltpu.make_async_copy(
            q_hbm.at[:, h * dqk:(h + 1) * dqk], q_v.at[h], in_sem.at[3 + 3 * h])
        loads.append((kc, vc, qc))
    for h in range(hh):
        loads[h][0].start()
        loads[h][1].start()

    barrier = pltpu.get_barrier_semaphore()
    for d in range(1, nh):
        pl.semaphore_signal(barrier, inc=1, device_id=(c, lax.rem(hd + d, nh)), device_id_type=MESH)
    for d in range(1, nc):
        pl.semaphore_signal(barrier, inc=1, device_id=(lax.rem(c + d, nc), hd), device_id_type=MESH)
    g_copy.wait()
    for p in range(nh):
        gsend[p, 0:hh, :] = g_v[0, p * hh:(p + 1) * hh, :]
        gsend[p, hh:2 * hh, :] = g_v[1, p * hh:(p + 1) * hh, :]
    pl.semaphore_wait(barrier, nh - 1 + nc - 1)

    def gate_copy(d):
        to = lax.rem(hd + d, nh)
        return pltpu.make_async_remote_copy(
            src_ref=gsend.at[to], dst_ref=grecv.at[hd], send_sem=gs_sem.at[d],
            recv_sem=gr_sem.at[d], device_id=(c, to), device_id_type=MESH)

    def gate_wait(d):
        frm = lax.rem(hd + nh - d, nh)
        return pltpu.make_async_remote_copy(
            src_ref=gsend.at[frm], dst_ref=grecv.at[frm], send_sem=gs_sem.at[d],
            recv_sem=gr_sem.at[d], device_id=(c, frm), device_id_type=MESH)

    for d in range(1, nh):
        gate_copy(d).start()
    grecv[hd] = gsend[hd]
    for h in range(hh):
        loads[h][0].wait()
        for j in range(nh):
            kt_v[j * hh + h] = (k_v[h, j * L:(j + 1) * L, :] * jnp.asarray(scale, BF16)).T
        loads[h][2].start()
    for d in range(1, nh):
        gate_wait(d).wait_recv()
    for p in range(nh):
        ig_s[p * hh:(p + 1) * hh, :] = grecv[p, 0:hh, :]
        fg_s[p * hh:(p + 1) * hh, :] = grecv[p, hh:2 * hh, :]
    ig = ig_s[...]
    fg = fg_s[...]
    logf = jnp.minimum(fg, 0.0) - jnp.log1p(jnp.exp(-jnp.abs(fg)))
    lane = lax.broadcasted_iota(jnp.int32, (nt, L), 1)
    cum = logf
    k = 1
    while k < L:
        cum = cum + shifted(cum, k, lane, 0.0)
        k *= 2
    a = ig - cum
    gb = jnp.broadcast_to(cum[:, L - 1:L], (nt, 128))
    ab = jnp.broadcast_to(jnp.max(a, axis=1, keepdims=True), (nt, 128))
    sl = jnp.full((hh, 128), NEG, F32)
    cg = jnp.zeros((hh, 128), F32)
    before, after, gone, keep = [], [], [], []
    for j in range(nh):
        gj = gb[j * hh:(j + 1) * hh]
        new = gj + jnp.maximum(sl, ab[j * hh:(j + 1) * hh])
        before.append(sl)
        gone.append(cg)
        keep.append(jnp.exp(gj + sl - new))
        sl = new
        cg = cg + gj
        after.append(sl)
    slp8 = jnp.concatenate(before, axis=0)
    cg8 = jnp.concatenate(gone, axis=0)
    w = jnp.exp(a + (gb - jnp.concatenate(after, axis=0))[:, 0:1])
    for r in range(nt):
        a3[r] = a[r:r + 1, :]
        w3[r] = w[r:r + 1, :]
        slp3[r] = slp8[r:r + 1, :]

    def s_copy(u):
        return pltpu.make_async_remote_copy(
            src_ref=sbuf.at[1 - x, u], dst_ref=srecv.at[u], send_sem=xs_sem.at[u],
            recv_sem=xr_sem.at[u], device_id=(2 * i + 1 - x, hd), device_id_type=MESH)

    def sum_copy(d, slot):
        return pltpu.make_async_remote_copy(
            src_ref=summ.at[slot], dst_ref=summ.at[slot], send_sem=ss_sem.at[d],
            recv_sem=sr_sem.at[d], device_id=(lax.rem(c + d, nc), hd), device_id_type=MESH)

    for h in range(hh):
        norm8[h:h + 1, :] = jnp.zeros((1, dqk), F32)
        run = None
        for j in range(nh):
            r = j * hh + h
            kw = kt_v[r].astype(F32) * w3[r]
            part = kw[:, 0:128]
            for b in range(1, L // 128):
                part = part + kw[:, b * 128:(b + 1) * 128]
            nrow = jnp.sum(part.T, axis=0, keepdims=True)
            kw_v[r] = kw.astype(BF16)
            run = nrow if j == 0 else nrow + keep[j][h:h + 1, 0:1] * run
            if j < nh - 1:
                norm8[r + hh:r + hh + 1, :] = run
            else:
                summ[c, h:h + 1, :] = run
    wide = jnp.ones((1, dqk), F32)
    summ[c, hh:2 * hh, :] = cg[:, 0:1] * wide
    summ[c, 2 * hh:3 * hh, :] = sl[:, 0:1] * wide
    for d in range(1, nc):
        sum_copy(d, c).start()

    for h in range(hh):
        loads[h][1].wait()
        mst[h] = jnp.zeros((dqk, dv), BF16)
        for j in range(nh):
            r = j * hh + h
            upd = jnp.dot(kw_v[r], v_v[h, j * L:(j + 1) * L, :], preferred_element_type=F32)
            if j > 0:
                upd = upd + keep[j][h:h + 1, 0:1] * st[...]
            if j < nh - 1:
                st[...] = upd
                mst[r + hh] = upd.astype(BF16)
            else:
                for cc in range(cph):
                    for b in range(pairs):
                        for xx in range(2):
                            r0 = (2 * b + xx) * R
                            sbuf[xx, h * cph + cc, b * R:(b + 1) * R, :] = upd[
                                r0:r0 + R, cc * CW:(cc + 1) * CW]
                    s_copy(h * cph + cc).start()

    amax_run = a
    k = 1
    while k < L:
        amax_run = jnp.maximum(amax_run, shifted(amax_run, k, lane, NEG))
        k *= 2

    @pl.when(i == 0)
    def _():
        erecv[...] = jnp.zeros(erecv.shape, F32)

    @pl.when(c == 0)
    def _():
        xrecv[...] = jnp.zeros(xrecv.shape, F32)

    for d in range(1, nc):
        sum_copy(d, lax.rem(c + nc - d, nc)).wait_recv()

    stab = jnp.full((hh, dqk), NEG, F32)
    norm = jnp.zeros((hh, dqk), F32)
    zero = jnp.zeros((hh, dqk), F32)
    in_stab, in_norm = zero, zero
    fa = [zero, zero, zero, zero]
    for s in range(nc):
        total = summ[s, hh:2 * hh, :]
        late = summ[s, 2 * hh:3 * hh, :]
        in_stab = jnp.where(c == s, stab, in_stab)
        in_norm = jnp.where(c == s, norm, in_norm)
        new = jnp.maximum(stab + total, late)
        fe = jnp.exp(stab + total - new)
        fl = jnp.exp(late - new)
        o = 2 * (s % 2)
        fa[o] = jnp.where(i == s // 2, fe, fa[o])
        fa[o + 1] = jnp.where(i == s // 2, fl, fa[o + 1])
        norm = fe * norm + fl * summ[s, 0:hh, :]
        stab = new
    norm_out[...] = norm
    max_out[...] = stab[:, 0:128]
    for h in range(hh):
        for o in range(4):
            fac[h, o:o + 1, :] = fa[o][h:h + 1, 0:128]
    insr8 = jnp.concatenate([in_stab[:, 0:128]] * nh, axis=0) + cg8
    sg8 = jnp.maximum(slp8, insr8)
    m = jnp.maximum(amax_run, sg8[:, 0:1])
    ng = (jnp.exp(slp8 - sg8)[:, 0:1] * norm8[...]
          + jnp.exp(insr8 - sg8)[:, 0:1] * jnp.concatenate([in_norm] * nh, axis=0))
    mt = m.T
    for r in range(nt):
        insr3[r] = insr8[r:r + 1, :]
        sg3[r] = sg8[r:r + 1, :]
        ng3[r] = ng[r:r + 1, :]
        mcolb[r] = jnp.broadcast_to(mt[:, r:r + 1], (L, 128))
    for h in range(hh):
        loads[h][2].wait()

    tt = min(256, L)

    tri = (lax.broadcasted_iota(jnp.int32, (tt, 128), 0)
           - lax.broadcasted_iota(jnp.int32, (tt, 128), 1))

    def intra(task, carry):
        h = task // nh
        j = task - h * nh
        r = j * hh + h
        base = pl.multiple_of(j * L, L)
        for rt in range(L // tt):
            t0 = rt * tt
            ncol = t0 + tt
            rows = pl.ds(pl.multiple_of(base + t0, tt), tt)
            q = q_v[h, rows, :]
            mc = mcolb[r, t0:t0 + tt, :]
            s = jnp.dot(q, kt_v[r, :, 0:ncol], preferred_element_type=F32)
            qf = q.astype(F32)
            ar, ng = a3[r], ng3[r]
            qn = qf[:, 0:128] * ng[:, 0:128]
            for b in range(1, dqk // 128):
                qn = qn + qf[:, b * 128:(b + 1) * 128] * ng[:, b * 128:(b + 1) * 128]
            den = jnp.exp(sg3[r] - mc) * qn
            mixed = []
            for b in range(ncol // 128):
                e = jnp.exp(ar[:, b * 128:(b + 1) * 128] - mc)
                if b * 128 >= t0:
                    e = jnp.where(tri + t0 >= b * 128, e, 0.0)
                e = e * s[:, b * 128:(b + 1) * 128]
                den = den + e
                mixed.append(e.astype(BF16))
            den = jnp.sum(den, axis=1, keepdims=True)
            inv = jnp.broadcast_to(1.0 / jnp.maximum(jnp.abs(den), 1.0), (tt, 128))
            num = jnp.dot(jnp.concatenate(mixed, axis=1), v_v[h, pl.ds(base, ncol), :],
                          preferred_element_type=F32)
            loc = jnp.dot(q, mst[r], preferred_element_type=F32)
            cl = jnp.exp(slp3[r] - mc) * inv
            ci = jnp.exp(insr3[r] - mc) * inv
            for b in range(dv // 128):
                cols = slice(b * 128, (b + 1) * 128)
                numv[h, rows, cols] = (num[:, cols] * inv + cl * loc[:, cols]).astype(BF16)
            for b in range(dqk // 128):
                cols = slice(b * 128, (b + 1) * 128)
                qsv[h, rows, cols] = (qf[:, cols] * ci).astype(BF16)
        return carry

    def e_copy(u):
        to = lax.rem(c + 2, nc)
        return pltpu.make_async_remote_copy(
            src_ref=eout.at[u], dst_ref=erecv.at[u], send_sem=es_sem.at[u],
            recv_sem=er_sem.at[u], device_id=(to, hd), device_id_type=MESH)

    def f_copy(u):
        return pltpu.make_async_remote_copy(
            src_ref=xsend.at[u], dst_ref=xrecv.at[u], send_sem=fs_sem.at[u],
            recv_sem=fr_sem.at[u], device_id=(2 * i + 1 - x, hd), device_id_type=MESH)

    def c_copy(u, b):
        return pltpu.make_async_remote_copy(
            src_ref=eout.at[u, pl.ds(b * R, R), :], dst_ref=closb.at[u],
            send_sem=cs_sem.at[u, b], recv_sem=cr_sem.at[u],
            device_id=(2 * b + x, hd), device_id_type=MESH)

    lead = jnp.minimum(i, nt // 2)

    def done(u):
        return jnp.minimum(lead + (u + 1) // 2, nt)

    def step(u, carry):
        lax.fori_loop(jnp.where(u == 0, 0, done(u - 1)), done(u), intra, 0)
        h = u // cph
        s_copy(u).wait_recv()

        @pl.when(i > 0)
        def _():
            e_copy(u).wait_recv()

        mine = sbuf[x, u]
        other = srecv[u]
        e = erecv[u]
        f = fac[h]
        first = jnp.where(x == 0, mine, other)
        second = jnp.where(x == 0, other, mine)
        mid = f[0:1, :] * e + f[1:2, :] * first
        eout[u] = f[2:3, :] * mid + f[3:4, :] * second
        xsend[u] = jnp.where(x == 0, mid, e)
        own[u] = jnp.where(x == 0, e, mid)

        @pl.when(i < pairs - 1)
        def _():
            e_copy(u).start()

        @pl.when(c != 1)
        def _():
            f_copy(u).start()

        @pl.when(i == pairs - 1)
        def _():
            for b in range(pairs - 1):
                c_copy(u, b).start()
            closb[u] = eout[u, (pairs - 1) * R:pairs * R, :]

        return carry

    lax.fori_loop(0, nu, step, 0)

    lax.fori_loop(done(nu - 1), nt, intra, 0)

    def gather(u, carry):
        @pl.when(c > 0)
        def _():
            f_copy(u).wait_recv()

        inm[:, x] = own[u].reshape(pairs, R, CW)
        inm[:, 1 - x] = xrecv[u].reshape(pairs, R, CW)
        mem_out[u] = inm[...].reshape(dqk, CW).astype(BF16)
        return carry

    lax.fori_loop(0, nu, gather, 0)

    for u in range(nu):
        @pl.when(i < pairs - 1)
        def _():
            c_copy(u, i).wait_recv()

        h, cc = u // cph, u % cph
        clos_out[h, :, cc * CW:(cc + 1) * CW] = closb[u]

    for d in range(1, nh):
        gate_copy(d).wait_send()
    for d in range(1, nc):
        sum_copy(d, c).wait_send()

    def drain(u, carry):
        s_copy(u).wait_send()

        @pl.when(i < pairs - 1)
        def _():
            e_copy(u).wait_send()

        @pl.when(c != 1)
        def _():
            f_copy(u).wait_send()

        @pl.when(i == pairs - 1)
        def _():
            for b in range(pairs - 1):
                c_copy(u, b).wait_send()

        return carry

    lax.fori_loop(0, nu, drain, 0)


def readout(hh, cph, num_ref, qs_ref, mem_ref, clos_in, norm_in, max_in,
            out_ref, clos_out, norm_out, max_out):
    dv = cph * CW
    tb = out_ref.shape[0]
    rows = pl.ds(pl.multiple_of(pl.program_id(0) * tb, tb), tb)
    for h in range(hh):
        mem = jnp.concatenate([mem_ref[h * cph + cc] for cc in range(cph)], axis=1)
        got = jnp.dot(qs_ref[h, rows, :], mem, preferred_element_type=F32)
        out_ref[:, h * dv:(h + 1) * dv] = (num_ref[h, rows, :].astype(F32) + got).astype(BF16)

    @pl.when(pl.program_id(0) == 0)
    def _():
        clos_out[...] = clos_in[...]
        norm_out[...] = norm_in[...]
        for h in range(hh):
            max_out[h] = max_in[h, 0]


def on_device(nc, nh, queries, keys, values, gate_pre):
    toks = queries.shape[0]
    hh = gate_pre.shape[1] // nh
    dqk = queries.shape[1] // hh
    dv = values.shape[1] // hh
    L = toks // nh
    R = dqk // nc
    pairs = nc // 2
    nu = hh * dv // CW
    nt = hh * nh
    half = dqk // 2
    vm = pltpu.VMEM
    dma = pltpu.SemaphoreType.DMA
    anyspec = pl.BlockSpec(memory_space=pl.ANY)
    vspec = pl.BlockSpec(memory_space=pltpu.VMEM)
    macs = hh * toks * (L * (dqk + dv) + 3 * dqk * dv)
    queries, keys, values, gate_pre = (
        pltpu.with_memory_space_constraint(t, pltpu.HBM) for t in (queries, keys, values, gate_pre))
    num, qs, mem, closing, norm, top = pl.pallas_call(
        functools.partial(kernel, nc, nh, hh, toks, dqk, dv),
        out_shape=(
            vm((hh, toks, dv), BF16),
            vm((hh, toks, dqk), BF16),
            vm((nu, dqk, CW), BF16),
            jax.ShapeDtypeStruct((hh, R, dv), F32),
            jax.ShapeDtypeStruct((hh, dqk), F32),
            jax.ShapeDtypeStruct((hh, 128), F32),
        ),
        in_specs=[anyspec] * 4,
        out_specs=(vspec,) * 6,
        scratch_shapes=[
            vm((hh, toks, dqk), BF16), vm((hh, toks, dqk), BF16), vm((hh, toks, dv), BF16),
            vm(gate_pre.shape, F32), vm((nh, 8, L), F32), vm((nh, 8, L), F32),
            vm((nt, L), F32), vm((nt, L), F32), vm((nt, dqk, L), BF16), vm((nt, dqk, L), BF16),
            vm((nt, 1, L), F32), vm((nt, L, 128), F32), vm((nt, 1, L), F32),
            vm((nt, 1, 128), F32), vm((nt, 1, 128), F32), vm((nt, 1, 128), F32),
            vm((nt, 1, dqk), F32), vm((nt, dqk), F32), vm((nt, dqk, dv), BF16),
            vm((dqk, dv), F32),
            vm((nc, 8, dqk), F32), vm((hh, 8, 128), F32),
            vm((2, nu, half, CW), F32), vm((nu, half, CW), F32), vm((nu, half, CW), F32),
            vm((nu, half, CW), F32), vm((nu, half, CW), F32), vm((nu, half, CW), F32),
            vm((nu, half, CW), F32), vm((nu, R, CW), F32), vm((pairs, 2, R, CW), F32),
            dma((1 + 3 * hh,)), dma((nh,)), dma((nh,)), dma((nc,)), dma((nc,)),
            dma((nu,)), dma((nu,)), dma((nu,)), dma((nu,)), dma((nu,)), dma((nu,)),
            dma((nu, pairs)), dma((nu,)),
        ],
        compiler_params=pltpu.CompilerParams(
            collective_id=0, has_side_effects=True, vmem_limit_bytes=54 * 1024 * 1024),
        cost_estimate=pl.CostEstimate(
            flops=2 * macs, bytes_accessed=12 * 1024 * 1024, transcendentals=hh * toks * L),
        name="mlstm",
    )(queries, keys, values, gate_pre)
    tb = min(256, toks)
    num = pltpu.with_memory_space_constraint(num, pltpu.VMEM)
    qs = pltpu.with_memory_space_constraint(qs, pltpu.VMEM)
    mem = pltpu.with_memory_space_constraint(mem, pltpu.VMEM)
    return pl.pallas_call(
        functools.partial(readout, hh, dv // CW),
        grid=(toks // tb,),
        out_shape=(
            jax.ShapeDtypeStruct((toks, hh * dv), BF16),
            jax.ShapeDtypeStruct((hh, R, dv), F32),
            jax.ShapeDtypeStruct((hh, dqk), F32),
            jax.ShapeDtypeStruct((hh,), F32),
        ),
        in_specs=[
            vspec, vspec, vspec, vspec, vspec, pl.BlockSpec(memory_space=pltpu.SMEM),
        ],
        out_specs=(
            pl.BlockSpec((tb, hh * dv), lambda t: (t, 0)),
            vspec, vspec, pl.BlockSpec(memory_space=pltpu.SMEM),
        ),
        compiler_params=pltpu.CompilerParams(vmem_limit_bytes=16 * 1024 * 1024),
        cost_estimate=pl.CostEstimate(
            flops=2 * hh * toks * dqk * dv, bytes_accessed=11 * 1024 * 1024, transcendentals=0),
        name="readout",
    )(num, qs, mem, closing, norm, top)


def solution(mesh):
    nc, nh = mesh.shape["ctx"], mesh.shape["head"]
    in_specs = (
        P("ctx", "head"),
        P("ctx", "head"),
        P("ctx", "head"),
        P(None, None, ("ctx", "head")),
    )
    out_specs = (P("ctx", "head"), P("head", "ctx", None), P("head", None), P("head"))
    return jax.shard_map(
        functools.partial(on_device, nc, nh),
        mesh=mesh, in_specs=in_specs, out_specs=out_specs, check_vma=False,
    )
```

```python
import functools

import jax
import jax.numpy as jnp
from jax import lax
from jax.experimental import pallas as pl
from jax.experimental.pallas import tpu as pltpu
from jax.sharding import PartitionSpec as P

NEG = -1e30
CW = 128
MESH = pl.DeviceIdType.MESH
F32 = jnp.float32
BF16 = jnp.bfloat16


def shifted(v, k, lane, fill):
    return jnp.where(lane >= k, pltpu.roll(v, k, axis=1), fill)


def kernel(
    nc, nh, hh, toks, dqk, dv,
    q_hbm, k_hbm, v_hbm, g_hbm,
    numv, qsv, mem_out, clos_out, norm_out, max_out,
    q_v, k_v, v_v, g_v, gsend, grecv, ig_s, fg_s, kt_v, kw_v,
    a3, mcolb, w3, slp3, insr3, sg3, ng3, norm8, mst, st,
    summ, fac, sbuf, srecv, erecv, eout, xsend, xrecv, own, closb, inm,
    in_sem, gs_sem, gr_sem, ss_sem, sr_sem, xs_sem, xr_sem,
    es_sem, er_sem, fs_sem, fr_sem, cs_sem, cr_sem,
):
    c = lax.axis_index("ctx")
    hd = lax.axis_index("head")
    i = c // 2
    x = c - 2 * i
    pairs = nc // 2
    L = toks // nh
    R = dqk // nc
    cph = dv // CW
    nu = hh * cph
    nt = hh * nh
    scale = dqk ** (-0.5)

    g_copy = pltpu.make_async_copy(g_hbm, g_v, in_sem.at[0])
    g_copy.start()
    loads = []
    for h in range(hh):
        kc = pltpu.make_async_copy(
            k_hbm.at[:, h * dqk:(h + 1) * dqk], k_v.at[h], in_sem.at[1 + 3 * h])
        vc = pltpu.make_async_copy(
            v_hbm.at[:, h * dv:(h + 1) * dv], v_v.at[h], in_sem.at[2 + 3 * h])
        qc = pltpu.make_async_copy(
            q_hbm.at[:, h * dqk:(h + 1) * dqk], q_v.at[h], in_sem.at[3 + 3 * h])
        loads.append((kc, vc, qc))
    for h in range(hh):
        loads[h][0].start()

    barrier = pltpu.get_barrier_semaphore()
    for d in range(1, nh):
        pl.semaphore_signal(barrier, inc=1, device_id=(c, lax.rem(hd + d, nh)), device_id_type=MESH)
    for d in range(1, nc):
        pl.semaphore_signal(barrier, inc=1, device_id=(lax.rem(c + d, nc), hd), device_id_type=MESH)
    g_copy.wait()
    for p in range(nh):
        gsend[p, 0:hh, :] = g_v[0, p * hh:(p + 1) * hh, :]
        gsend[p, hh:2 * hh, :] = g_v[1, p * hh:(p + 1) * hh, :]
    for h in range(hh):
        loads[h][1].start()
    pl.semaphore_wait(barrier, nh - 1 + nc - 1)

    def gate_copy(d):
        to = lax.rem(hd + d, nh)
        return pltpu.make_async_remote_copy(
            src_ref=gsend.at[to], dst_ref=grecv.at[hd], send_sem=gs_sem.at[d],
            recv_sem=gr_sem.at[d], device_id=(c, to), device_id_type=MESH)

    def gate_wait(d):
        frm = lax.rem(hd + nh - d, nh)
        return pltpu.make_async_remote_copy(
            src_ref=gsend.at[frm], dst_ref=grecv.at[frm], send_sem=gs_sem.at[d],
            recv_sem=gr_sem.at[d], device_id=(c, frm), device_id_type=MESH)

    for d in range(1, nh):
        gate_copy(d).start()
    grecv[hd] = gsend[hd]
    for h in range(hh):
        loads[h][0].wait()
        for j in range(nh):
            kt_v[j * hh + h] = (k_v[h, j * L:(j + 1) * L, :] * jnp.asarray(scale, BF16)).T
        loads[h][2].start()
    for d in range(1, nh):
        gate_wait(d).wait_recv()
    for p in range(nh):
        ig_s[p * hh:(p + 1) * hh, :] = grecv[p, 0:hh, :]
        fg_s[p * hh:(p + 1) * hh, :] = grecv[p, hh:2 * hh, :]
    ig = ig_s[...]
    fg = fg_s[...]
    logf = jnp.minimum(fg, 0.0) - jnp.log1p(jnp.exp(-jnp.abs(fg)))
    lane = lax.broadcasted_iota(jnp.int32, (nt, L), 1)
    cum = logf
    k = 1
    while k < L:
        cum = cum + shifted(cum, k, lane, 0.0)
        k *= 2
    a = ig - cum
    gb = jnp.broadcast_to(cum[:, L - 1:L], (nt, 128))
    ab = jnp.broadcast_to(jnp.max(a, axis=1, keepdims=True), (nt, 128))
    sl = jnp.full((hh, 128), NEG, F32)
    cg = jnp.zeros((hh, 128), F32)
    before, after, gone, keep = [], [], [], []
    for j in range(nh):
        gj = gb[j * hh:(j + 1) * hh]
        new = gj + jnp.maximum(sl, ab[j * hh:(j + 1) * hh])
        before.append(sl)
        gone.append(cg)
        keep.append(jnp.exp(gj + sl - new))
        sl = new
        cg = cg + gj
        after.append(sl)
    slp8 = jnp.concatenate(before, axis=0)
    cg8 = jnp.concatenate(gone, axis=0)
    w = jnp.exp(a + (gb - jnp.concatenate(after, axis=0))[:, 0:1])
    for r in range(nt):
        a3[r] = a[r:r + 1, :]
        w3[r] = w[r:r + 1, :]
        slp3[r] = slp8[r:r + 1, :]

    def s_copy(u):
        return pltpu.make_async_remote_copy(
            src_ref=sbuf.at[1 - x, u], dst_ref=srecv.at[u], send_sem=xs_sem.at[u],
            recv_sem=xr_sem.at[u], device_id=(2 * i + 1 - x, hd), device_id_type=MESH)

    def sum_copy(d, slot):
        return pltpu.make_async_remote_copy(
            src_ref=summ.at[slot], dst_ref=summ.at[slot], send_sem=ss_sem.at[d],
            recv_sem=sr_sem.at[d], device_id=(lax.rem(c + d, nc), hd), device_id_type=MESH)

    for h in range(hh):
        norm8[h:h + 1, :] = jnp.zeros((1, dqk), F32)
        run = None
        for j in range(nh):
            r = j * hh + h
            kw = kt_v[r].astype(F32) * w3[r]
            part = kw[:, 0:128]
            for b in range(1, L // 128):
                part = part + kw[:, b * 128:(b + 1) * 128]
            nrow = jnp.sum(part.T, axis=0, keepdims=True)
            kw_v[r] = kw.astype(BF16)
            run = nrow if j == 0 else nrow + keep[j][h:h + 1, 0:1] * run
            if j < nh - 1:
                norm8[r + hh:r + hh + 1, :] = run
            else:
                summ[c, h:h + 1, :] = run
    wide = jnp.ones((1, dqk), F32)
    summ[c, hh:2 * hh, :] = cg[:, 0:1] * wide
    summ[c, 2 * hh:3 * hh, :] = sl[:, 0:1] * wide
    for d in range(1, nc):
        sum_copy(d, c).start()

    for h in range(hh):
        loads[h][1].wait()
        mst[h] = jnp.zeros((dqk, dv), BF16)
        for j in range(nh):
            r = j * hh + h
            upd = jnp.dot(kw_v[r], v_v[h, j * L:(j + 1) * L, :], preferred_element_type=F32)
            if j > 0:
                upd = upd + keep[j][h:h + 1, 0:1] * st[...]
            if j < nh - 1:
                st[...] = upd
                mst[r + hh] = upd.astype(BF16)
            else:
                for cc in range(cph):
                    for b in range(pairs):
                        for xx in range(2):
                            r0 = (2 * b + xx) * R
                            sbuf[xx, h * cph + cc, b * R:(b + 1) * R, :] = upd[
                                r0:r0 + R, cc * CW:(cc + 1) * CW]
                    s_copy(h * cph + cc).start()

    amax_run = a
    k = 1
    while k < L:
        amax_run = jnp.maximum(amax_run, shifted(amax_run, k, lane, NEG))
        k *= 2

    @pl.when(i == 0)
    def _():
        erecv[...] = jnp.zeros(erecv.shape, F32)

    @pl.when(c == 0)
    def _():
        xrecv[...] = jnp.zeros(xrecv.shape, F32)

    for d in range(1, nc):
        sum_copy(d, lax.rem(c + nc - d, nc)).wait_recv()

    stab = jnp.full((hh, dqk), NEG, F32)
    norm = jnp.zeros((hh, dqk), F32)
    zero = jnp.zeros((hh, dqk), F32)
    in_stab, in_norm = zero, zero
    fa = [zero, zero, zero, zero]
    for s in range(nc):
        total = summ[s, hh:2 * hh, :]
        late = summ[s, 2 * hh:3 * hh, :]
        in_stab = jnp.where(c == s, stab, in_stab)
        in_norm = jnp.where(c == s, norm, in_norm)
        new = jnp.maximum(stab + total, late)
        fe = jnp.exp(stab + total - new)
        fl = jnp.exp(late - new)
        o = 2 * (s % 2)
        fa[o] = jnp.where(i == s // 2, fe, fa[o])
        fa[o + 1] = jnp.where(i == s // 2, fl, fa[o + 1])
        norm = fe * norm + fl * summ[s, 0:hh, :]
        stab = new
    norm_out[...] = norm
    max_out[...] = stab[:, 0:128]
    for h in range(hh):
        for o in range(4):
            fac[h, o:o + 1, :] = fa[o][h:h + 1, 0:128]
    insr8 = jnp.concatenate([in_stab[:, 0:128]] * nh, axis=0) + cg8
    sg8 = jnp.maximum(slp8, insr8)
    m = jnp.maximum(amax_run, sg8[:, 0:1])
    ng = (jnp.exp(slp8 - sg8)[:, 0:1] * norm8[...]
          + jnp.exp(insr8 - sg8)[:, 0:1] * jnp.concatenate([in_norm] * nh, axis=0))
    mt = m.T
    for r in range(nt):
        insr3[r] = insr8[r:r + 1, :]
        sg3[r] = sg8[r:r + 1, :]
        ng3[r] = ng[r:r + 1, :]
        mcolb[r] = jnp.broadcast_to(mt[:, r:r + 1], (L, 128))
    for h in range(hh):
        loads[h][2].wait()

    tt = min(256, L)

    tri = (lax.broadcasted_iota(jnp.int32, (tt, 128), 0)
           - lax.broadcasted_iota(jnp.int32, (tt, 128), 1))

    def intra(task, carry):
        h = task // nh
        j = task - h * nh
        r = j * hh + h
        base = pl.multiple_of(j * L, L)
        for rt in range(L // tt):
            t0 = rt * tt
            ncol = t0 + tt
            rows = pl.ds(pl.multiple_of(base + t0, tt), tt)
            q = q_v[h, rows, :]
            mc = mcolb[r, t0:t0 + tt, :]
            s = jnp.dot(q, kt_v[r, :, 0:ncol], preferred_element_type=F32)
            qf = q.astype(F32)
            ar, ng = a3[r], ng3[r]
            qn = qf[:, 0:128] * ng[:, 0:128]
            for b in range(1, dqk // 128):
                qn = qn + qf[:, b * 128:(b + 1) * 128] * ng[:, b * 128:(b + 1) * 128]
            den = jnp.exp(sg3[r] - mc) * qn
            mixed = []
            for b in range(ncol // 128):
                e = jnp.exp(ar[:, b * 128:(b + 1) * 128] - mc)
                if b * 128 >= t0:
                    e = jnp.where(tri + t0 >= b * 128, e, 0.0)
                e = e * s[:, b * 128:(b + 1) * 128]
                den = den + e
                mixed.append(e.astype(BF16))
            den = jnp.sum(den, axis=1, keepdims=True)
            inv = jnp.broadcast_to(1.0 / jnp.maximum(jnp.abs(den), 1.0), (tt, 128))
            num = jnp.dot(jnp.concatenate(mixed, axis=1), v_v[h, pl.ds(base, ncol), :],
                          preferred_element_type=F32)
            loc = jnp.dot(q, mst[r], preferred_element_type=F32)
            cl = jnp.exp(slp3[r] - mc) * inv
            ci = jnp.exp(insr3[r] - mc) * inv
            for b in range(dv // 128):
                cols = slice(b * 128, (b + 1) * 128)
                numv[h, rows, cols] = (num[:, cols] * inv + cl * loc[:, cols]).astype(BF16)
            for b in range(dqk // 128):
                cols = slice(b * 128, (b + 1) * 128)
                qsv[h, rows, cols] = (qf[:, cols] * ci).astype(BF16)
        return carry

    def e_copy(u):
        to = lax.rem(c + 2, nc)
        return pltpu.make_async_remote_copy(
            src_ref=eout.at[u], dst_ref=erecv.at[u], send_sem=es_sem.at[u],
            recv_sem=er_sem.at[u], device_id=(to, hd), device_id_type=MESH)

    def f_copy(u):
        return pltpu.make_async_remote_copy(
            src_ref=xsend.at[u], dst_ref=xrecv.at[u], send_sem=fs_sem.at[u],
            recv_sem=fr_sem.at[u], device_id=(2 * i + 1 - x, hd), device_id_type=MESH)

    def c_copy(u, b):
        return pltpu.make_async_remote_copy(
            src_ref=eout.at[u, pl.ds(b * R, R), :], dst_ref=closb.at[u],
            send_sem=cs_sem.at[u, b], recv_sem=cr_sem.at[u],
            device_id=(2 * b + x, hd), device_id_type=MESH)

    lead = jnp.minimum(i, nt // 2)

    def done(u):
        return jnp.minimum(lead + (u + 1) // 2, nt)

    def step(u, carry):
        lax.fori_loop(jnp.where(u == 0, 0, done(u - 1)), done(u), intra, 0)
        h = u // cph
        s_copy(u).wait_recv()

        @pl.when(i > 0)
        def _():
            e_copy(u).wait_recv()

        mine = sbuf[x, u]
        other = srecv[u]
        e = erecv[u]
        f = fac[h]
        first = jnp.where(x == 0, mine, other)
        second = jnp.where(x == 0, other, mine)
        mid = f[0:1, :] * e + f[1:2, :] * first
        eout[u] = f[2:3, :] * mid + f[3:4, :] * second
        xsend[u] = jnp.where(x == 0, mid, e)
        own[u] = jnp.where(x == 0, e, mid)

        @pl.when(i < pairs - 1)
        def _():
            e_copy(u).start()

        @pl.when(c != 1)
        def _():
            f_copy(u).start()

        @pl.when(i == pairs - 1)
        def _():
            for b in range(pairs - 1):
                c_copy(u, b).start()
            closb[u] = eout[u, (pairs - 1) * R:pairs * R, :]

        return carry

    lax.fori_loop(0, nu, step, 0)

    lax.fori_loop(done(nu - 1), nt, intra, 0)

    def gather(u, carry):
        @pl.when(c > 0)
        def _():
            f_copy(u).wait_recv()

        inm[:, x] = own[u].reshape(pairs, R, CW)
        inm[:, 1 - x] = xrecv[u].reshape(pairs, R, CW)
        mem_out[u] = inm[...].reshape(dqk, CW).astype(BF16)
        return carry

    lax.fori_loop(0, nu, gather, 0)

    for u in range(nu):
        @pl.when(i < pairs - 1)
        def _():
            c_copy(u, i).wait_recv()

        h, cc = u // cph, u % cph
        clos_out[h, :, cc * CW:(cc + 1) * CW] = closb[u]

    for d in range(1, nh):
        gate_copy(d).wait_send()
    for d in range(1, nc):
        sum_copy(d, c).wait_send()

    def drain(u, carry):
        s_copy(u).wait_send()

        @pl.when(i < pairs - 1)
        def _():
            e_copy(u).wait_send()

        @pl.when(c != 1)
        def _():
            f_copy(u).wait_send()

        @pl.when(i == pairs - 1)
        def _():
            for b in range(pairs - 1):
                c_copy(u, b).wait_send()

        return carry

    lax.fori_loop(0, nu, drain, 0)


def readout(hh, cph, num_ref, qs_ref, mem_ref, clos_in, norm_in, max_in,
            out_ref, clos_out, norm_out, max_out):
    dv = cph * CW
    tb = out_ref.shape[0]
    rows = pl.ds(pl.multiple_of(pl.program_id(0) * tb, tb), tb)
    for h in range(hh):
        mem = jnp.concatenate([mem_ref[h * cph + cc] for cc in range(cph)], axis=1)
        got = jnp.dot(qs_ref[h, rows, :], mem, preferred_element_type=F32)
        out_ref[:, h * dv:(h + 1) * dv] = (num_ref[h, rows, :].astype(F32) + got).astype(BF16)

    @pl.when(pl.program_id(0) == 0)
    def _():
        clos_out[...] = clos_in[...]
        norm_out[...] = norm_in[...]
        for h in range(hh):
            max_out[h] = jnp.max(max_in[h:h + 1, :])


def on_device(nc, nh, queries, keys, values, gate_pre):
    toks = queries.shape[0]
    hh = gate_pre.shape[1] // nh
    dqk = queries.shape[1] // hh
    dv = values.shape[1] // hh
    L = toks // nh
    R = dqk // nc
    pairs = nc // 2
    nu = hh * dv // CW
    nt = hh * nh
    half = dqk // 2
    vm = pltpu.VMEM
    dma = pltpu.SemaphoreType.DMA
    anyspec = pl.BlockSpec(memory_space=pl.ANY)
    vspec = pl.BlockSpec(memory_space=pltpu.VMEM)
    macs = hh * toks * (L * (dqk + dv) + 3 * dqk * dv)
    queries, keys, values, gate_pre = (
        pltpu.with_memory_space_constraint(t, pltpu.HBM) for t in (queries, keys, values, gate_pre))
    num, qs, mem, closing, norm, top = pl.pallas_call(
        functools.partial(kernel, nc, nh, hh, toks, dqk, dv),
        out_shape=(
            vm((hh, toks, dv), BF16),
            vm((hh, toks, dqk), BF16),
            vm((nu, dqk, CW), BF16),
            vm((hh, R, dv), F32),
            vm((hh, dqk), F32),
            vm((hh, 128), F32),
        ),
        in_specs=[anyspec] * 4,
        out_specs=(vspec,) * 6,
        scratch_shapes=[
            vm((hh, toks, dqk), BF16), vm((hh, toks, dqk), BF16), vm((hh, toks, dv), BF16),
            vm(gate_pre.shape, F32), vm((nh, 8, L), F32), vm((nh, 8, L), F32),
            vm((nt, L), F32), vm((nt, L), F32), vm((nt, dqk, L), BF16), vm((nt, dqk, L), BF16),
            vm((nt, 1, L), F32), vm((nt, L, 128), F32), vm((nt, 1, L), F32),
            vm((nt, 1, 128), F32), vm((nt, 1, 128), F32), vm((nt, 1, 128), F32),
            vm((nt, 1, dqk), F32), vm((nt, dqk), F32), vm((nt, dqk, dv), BF16),
            vm((dqk, dv), F32),
            vm((nc, 8, dqk), F32), vm((hh, 8, 128), F32),
            vm((2, nu, half, CW), F32), vm((nu, half, CW), F32), vm((nu, half, CW), F32),
            vm((nu, half, CW), F32), vm((nu, half, CW), F32), vm((nu, half, CW), F32),
            vm((nu, half, CW), F32), vm((nu, R, CW), F32), vm((pairs, 2, R, CW), F32),
            dma((1 + 3 * hh,)), dma((nh,)), dma((nh,)), dma((nc,)), dma((nc,)),
            dma((nu,)), dma((nu,)), dma((nu,)), dma((nu,)), dma((nu,)), dma((nu,)),
            dma((nu, pairs)), dma((nu,)),
        ],
        compiler_params=pltpu.CompilerParams(
            collective_id=0, has_side_effects=True, vmem_limit_bytes=54 * 1024 * 1024),
        cost_estimate=pl.CostEstimate(
            flops=2 * macs, bytes_accessed=12 * 1024 * 1024, transcendentals=hh * toks * L),
        name="mlstm",
    )(queries, keys, values, gate_pre)
    tb = min(512, toks)
    num, qs, mem, closing, norm, top = (
        pltpu.with_memory_space_constraint(t, pltpu.VMEM)
        for t in (num, qs, mem, closing, norm, top))
    return pl.pallas_call(
        functools.partial(readout, hh, dv // CW),
        grid=(toks // tb,),
        out_shape=(
            jax.ShapeDtypeStruct((toks, hh * dv), BF16),
            jax.ShapeDtypeStruct((hh, R, dv), F32),
            jax.ShapeDtypeStruct((hh, dqk), F32),
            jax.ShapeDtypeStruct((hh,), F32),
        ),
        in_specs=[
            vspec, vspec, vspec, vspec, vspec, vspec,
        ],
        out_specs=(
            pl.BlockSpec((tb, hh * dv), lambda t: (t, 0)),
            vspec, vspec, pl.BlockSpec(memory_space=pltpu.SMEM),
        ),
        compiler_params=pltpu.CompilerParams(vmem_limit_bytes=16 * 1024 * 1024),
        cost_estimate=pl.CostEstimate(
            flops=2 * hh * toks * dqk * dv, bytes_accessed=11 * 1024 * 1024, transcendentals=0),
        name="readout",
    )(num, qs, mem, closing, norm, top)


def solution(mesh):
    nc, nh = mesh.shape["ctx"], mesh.shape["head"]
    in_specs = (
        P("ctx", "head"),
        P("ctx", "head"),
        P("ctx", "head"),
        P(None, None, ("ctx", "head")),
    )
    out_specs = (P("ctx", "head"), P("head", "ctx", None), P("head", None), P("head"))
    return jax.shard_map(
        functools.partial(on_device, nc, nh),
        mesh=mesh, in_specs=in_specs, out_specs=out_specs, check_vma=False,
    )
```
